32 devices in a mesh: pop: 2 (over y), hid: 8 (over z, x), tok: 2 (over core).
Axes of the slice: x: 2, y: 2, z: 4, core: 2. Of those that a mesh axis runs over, the one named last changes fastest.
Arguments:
- tokens: bfloat16 [3072, 8192], P(('pop', 'tok'), 'hid'), parts along dimension 0, may hold values from -6 to 6
- teacher: bfloat16 [3072, 8192], P(('pop', 'tok'), 'hid'), parts along dimension 0, may hold values from -8 to 8
- assigned: int32 [3072], P(('pop', 'tok')), parts along dimension 0, may hold values 0 or 1
- bfly_in: bfloat16 [256, 8, 64, 256], P(('pop', 'hid')), parts along dimension 0, may hold values from -0.25 to 0.25
- bfly_out: bfloat16 [256, 8, 256, 64], P(('pop', 'hid')), parts along dimension 0, may hold values from -0.125 to 0.125
- low_in_a: bfloat16 [16384, 512], P(('pop', 'hid')), parts along dimension 0, may hold values from -0.0625 to 0.0625
- low_in_b: bfloat16 [1024, 32768], P('pop', 'hid'), parts along dimension 0, may hold values from -0.25 to 0.25
- low_out_a: bfloat16 [65536, 512], P(('pop', 'hid')), parts along dimension 0, may hold values from -0.03125 to 0.03125
- low_out_b: bfloat16 [1024, 8192], P('pop', 'hid'), parts along dimension 0, may hold values from -0.25 to 0.25
- hidden_order: int32 [128, 256], P('hid'), may hold values from 0 to 255, each once within a row
Outputs:
- student: bfloat16 [3072, 8192], P(('pop', 'tok'), 'hid'), parts along dimension 0
- grad_tokens: bfloat16 [3072, 8192], P(('pop', 'tok'), 'hid'), parts along dimension 0
- grad_bfly_in: float32 [256, 8, 64, 256], P(('pop', 'hid'), None, None, 'tok'), parts along dimension 0
- grad_bfly_out: float32 [256, 8, 256, 64], P(('pop', 'hid'), None, 'tok'), parts along dimension 0
- grad_low_in_a: float32 [16384, 512], P(('pop', 'hid'), 'tok'), parts along dimension 0
- grad_low_in_b: float32 [1024, 32768], P(('pop', 'tok'), 'hid'), parts along dimension 0
- grad_low_out_a: float32 [65536, 512], P(('pop', 'hid'), 'tok'), parts along dimension 0
- grad_low_out_b: float32 [1024, 8192], P(('pop', 'tok'), 'hid'), parts along dimension 0
The draws below stay inside these ranges and needn't reach their ends.
There are 2 independent parts, one for each index of `pop`. The reference program is written for one: setup_inputs(seed, part) draws one part's arguments, and reference() takes and returns one part's arrays. A program takes and returns all parts, laid end to end along the dimension named above; an argument that names none is the same for every part. Nothing has to cross between parts.
Inputs may be any that keep to these rules, and one draw needn't show every extreme that they name: Each row of hidden_order holds every number 0 to 255 once.
All inputs are finite; a program needn't handle non-finite values. No bound on the sum of `assigned` on one device may be relied on, other than what follows from the above.
Results may differ from the reference program's by a relative error of at most 0.012.
Values may be sent and summed in bfloat16 or wider, within the bound.
A program may use at most 384 MiB of HBM per device.

```python
import jax
import jax.numpy as jnp
import numpy as np
from jax import lax

D = 8192
FF = 32768
BLK = 256
RANK = 512
LEVELS = 7
NB = 128
IB = 64
TOKENS = 1536


def place_ends(entries, rng, low, largest):
    spot = [jax.random.randint(jax.random.fold_in(rng, axis), (), 0, length) for axis, length in enumerate(entries.shape)]
    main_axis = entries.shape.index(max(entries.shape))
    next_to = spot[:main_axis] + [(spot[main_axis] + 1) % entries.shape[main_axis]] + spot[main_axis + 1:]
    return entries.at[tuple(spot)].set(low).at[tuple(next_to)].set(largest)


def block_scale(key, shape, cuts, low, top_value):
    def one(axis_at, shards_of):
        heights = jax.random.uniform(jax.random.fold_in(jax.random.fold_in(key, 6), axis_at), (shards_of,), jnp.float32, low / len(cuts), top_value / len(cuts))
        return jnp.repeat(jnp.exp(heights), shape[axis_at] // shards_of).reshape((-1,) + (1,) * (len(shape) - axis_at - 1))

    gain = one(*cuts[0])
    for cut in cuts[1:]:
        gain = gain * one(*cut)
    return gain


def scatter_about(rng, dims, spread, limit, pieces=(), held_as=jnp.bfloat16):
    drawn = spread * jax.random.normal(rng, dims, jnp.float32)
    if pieces:
        drawn = drawn * block_scale(rng, dims, pieces, -0.22, 0.18)
    return jnp.clip(drawn, -limit, limit).astype(held_as)


def setup_inputs(seed: int = 0, part: int = 0) -> dict:
    arg_keys = jax.random.split(jax.random.key(seed), 11)
    part_keys = jax.random.split(jax.random.fold_in(arg_keys[10], part), 11)
    tokens = scatter_about(part_keys[0], (TOKENS, D), 1.0, 6.0, ((0, 2), (1, 8)))
    teacher = scatter_about(part_keys[1], (TOKENS, D), 1.4, 8.0, ((0, 2), (1, 8)))
    assigned = place_ends((jax.random.randint(part_keys[2], (TOKENS,), 0, 4) < 3).astype(jnp.int32), jax.random.fold_in(part_keys[2], 1), 0, 1)
    bfly_in = scatter_about(part_keys[3], (NB, LEVELS + 1, IB, BLK), ((LEVELS + 1) * IB) ** -0.5, 0.25, ((0, 8),))
    bfly_out = scatter_about(part_keys[4], (NB, LEVELS + 1, BLK, IB), ((LEVELS + 1) * BLK) ** -0.5, 0.125, ((0, 8),))
    low_in_a = scatter_about(part_keys[5], (D, RANK), D ** -0.5, 0.0625, ((0, 8),))
    low_in_b = scatter_about(part_keys[6], (RANK, FF), RANK ** -0.5, 0.25, ((1, 8),))
    low_out_a = scatter_about(part_keys[7], (FF, RANK), FF ** -0.5, 0.03125, ((0, 8),))
    low_out_b = scatter_about(part_keys[8], (RANK, D), RANK ** -0.5, 0.25, ((1, 8),))
    hidden_order = jax.vmap(lambda own: jax.random.permutation(own, BLK))(jax.random.split(arg_keys[9], NB)).reshape((NB, BLK)).astype(jnp.int32)
    return dict(tokens=tokens, teacher=teacher, assigned=assigned, bfly_in=bfly_in, bfly_out=bfly_out, low_in_a=low_in_a, low_in_b=low_in_b, low_out_a=low_out_a, low_out_b=low_out_b, hidden_order=hidden_order)


inv_root_two = 0.7071067811865476
inv_root_tau = 0.3989422804014327


def stride_of(level_index):
    return 2 ** level_index if level_index < LEVELS else 0


def gelu_slope(values):
    return 0.5 * (1.0 + lax.erf(values * inv_root_two)) + values * jnp.exp(-0.5 * values * values) * inv_root_tau


def reference(tokens, teacher, assigned, bfly_in, bfly_out, low_in_a, low_in_b, low_out_a, low_out_b, hidden_order):
    count = tokens.shape[0]
    loss_scale = TOKENS ** -0.5
    blocks_in = tokens.reshape(count, NB, IB).astype(jnp.float32)
    tiles_in = bfly_in.astype(jnp.float32)
    tiles_out = bfly_out.astype(jnp.float32)
    orders = [np.arange(NB) ^ stride_of(level_index) for level_index in range(LEVELS + 1)]
    pre_act = jnp.zeros((count, NB, BLK), jnp.float32)
    for level_index in range(LEVELS + 1):
        source = blocks_in[:, orders[level_index]]
        pre_act = pre_act + jnp.einsum("tji,jio->tjo", source, tiles_in[:, level_index])
    low_first = jnp.dot(tokens, low_in_a, preferred_element_type=jnp.float32).astype(jnp.bfloat16)
    pre_act = pre_act + jnp.dot(low_first, low_in_b, preferred_element_type=jnp.float32).reshape(count, NB, BLK)
    activated = jax.nn.gelu(pre_act, approximate=False)
    order_table = hidden_order.astype(jnp.int32)
    hidden = jnp.take_along_axis(activated, order_table[None], axis=2).astype(jnp.bfloat16)
    hidden_wide = hidden.astype(jnp.float32)
    out_bfly = jnp.zeros((count, NB, IB), jnp.float32)
    for level_index in range(LEVELS + 1):
        partial_out = jnp.einsum("tjo,joi->tji", hidden_wide, tiles_out[:, level_index])
        out_bfly = out_bfly + partial_out[:, orders[level_index]]
    hidden_flat = hidden.reshape(count, FF)
    low_second = jnp.dot(hidden_flat, low_out_a, preferred_element_type=jnp.float32).astype(jnp.bfloat16)
    student = (out_bfly.reshape(count, D) + jnp.dot(low_second, low_out_b, preferred_element_type=jnp.float32)).astype(jnp.bfloat16)
    residual_grad = (assigned[:, None].astype(jnp.float32) * (student.astype(jnp.float32) - teacher.astype(jnp.float32))).astype(jnp.bfloat16)
    grad_blocks = residual_grad.reshape(count, NB, IB).astype(jnp.float32)
    hid_bfly = jnp.zeros((count, NB, BLK), jnp.float32)
    out_tiles = []
    for level_index in range(LEVELS + 1):
        source = grad_blocks[:, orders[level_index]]
        hid_bfly = hid_bfly + jnp.einsum("tji,joi->tjo", source, tiles_out[:, level_index])
        out_tiles.append(loss_scale * jnp.einsum("tjo,tji->joi", hidden_wide, source))
    grad_second = jnp.dot(residual_grad, low_out_b.T, preferred_element_type=jnp.float32).astype(jnp.bfloat16)
    hidden_grad = hid_bfly.reshape(count, FF) + jnp.dot(grad_second, low_out_a.T, preferred_element_type=jnp.float32)
    inverse_order = jnp.argsort(order_table, axis=1).astype(jnp.int32)
    act_grad = jnp.take_along_axis(hidden_grad.reshape(count, NB, BLK), inverse_order[None], axis=2)
    pre_grad = (act_grad * gelu_slope(pre_act)).astype(jnp.bfloat16)
    pre_wide = pre_grad.astype(jnp.float32)
    feat_bfly = jnp.zeros((count, NB, IB), jnp.float32)
    in_tiles = []
    for level_index in range(LEVELS + 1):
        partial_feat = jnp.einsum("tjo,jio->tji", pre_wide, tiles_in[:, level_index])
        feat_bfly = feat_bfly + partial_feat[:, orders[level_index]]
        source = blocks_in[:, orders[level_index]]
        in_tiles.append(loss_scale * jnp.einsum("tji,tjo->jio", source, pre_wide))
    pre_flat = pre_grad.reshape(count, FF)
    grad_first = jnp.dot(pre_flat, low_in_b.T, preferred_element_type=jnp.float32).astype(jnp.bfloat16)
    grad_tokens = (feat_bfly.reshape(count, D) + jnp.dot(grad_first, low_in_a.T, preferred_element_type=jnp.float32)).astype(jnp.bfloat16)
    grad_bfly_in = jnp.stack(in_tiles, axis=1)
    grad_bfly_out = jnp.stack(out_tiles, axis=1)
    grad_low_in_a = loss_scale * jnp.dot(tokens.T, grad_first, preferred_element_type=jnp.float32)
    grad_low_in_b = loss_scale * jnp.dot(low_first.T, pre_flat, preferred_element_type=jnp.float32)
    grad_low_out_a = loss_scale * jnp.dot(hidden_flat.T, grad_second, preferred_element_type=jnp.float32)
    grad_low_out_b = loss_scale * jnp.dot(low_second.T, residual_grad, preferred_element_type=jnp.float32)
    return (student, grad_tokens, grad_bfly_in, grad_bfly_out, grad_low_in_a, grad_low_in_b, grad_low_out_a, grad_low_out_b)
```

```python
import functools

import jax
import jax.numpy as jnp
from jax import lax
from jax.experimental import pallas as pl
from jax.experimental.pallas import tpu as pltpu
from jax.sharding import PartitionSpec as P

BLK = 256
LEVELS = 7
IB = 64
PAIR_IN = 2 * IB
PAIR_HID = 2 * BLK
SOURCES = LEVELS
LEVEL_ORDER = (LEVELS,) + tuple(range(1, LEVELS))
WIDE = SOURCES * PAIR_IN
VMEM_BYTES = 52 * 2**20

inv_root_two = 0.7071067811865476
inv_root_tau = 0.3989422804014327


def partner(value, axis, mask):
    pairs = [(source, source ^ mask) for source in range(lax.axis_size(axis))]
    return lax.ppermute(value, axis, pairs)


def dot(left, right, left_dim, right_dim):
    return lax.dot_general(
        left, right, (((left_dim,), (right_dim,)), ((), ())), preferred_element_type=jnp.float32
    )


def hid_sum(value):
    devices = lax.axis_size("hid")
    place = lax.axis_index("hid")
    masks = [2**bit for bit in range(devices.bit_length() - 1)]
    for mask in masks:
        low, high = jnp.split(value, 2, axis=0)
        upper = (place & mask) != 0
        kept = jnp.where(upper, high, low)
        sent = jnp.where(upper, low, high).astype(jnp.bfloat16)
        value = kept + partner(sent, "hid", mask).astype(jnp.float32)
    value = value.astype(jnp.bfloat16)
    for mask in reversed(masks):
        other = partner(value, "hid", mask)
        upper = (place & mask) != 0
        value = jnp.concatenate(
            [jnp.where(upper, other, value), jnp.where(upper, value, other)], axis=0
        )
    return value


def pair_weights(tiles):
    pairs = tiles.reshape((tiles.shape[0] // 2, 2) + tiles.shape[1:])
    straight = jnp.concatenate([pairs[:, :, LEVELS:], pairs[:, :, 1:LEVELS]], axis=2)
    cross = jnp.concatenate([pairs[:, :, :1], jnp.zeros_like(pairs[:, :, 1:LEVELS])], axis=2)
    return straight, cross


def input_weights(bfly_in):
    straight, cross = pair_weights(bfly_in)
    upper = jnp.concatenate([straight[:, 0], cross[:, 1]], axis=-1)
    lower = jnp.concatenate([cross[:, 0], straight[:, 1]], axis=-1)
    both = jnp.concatenate([upper, lower], axis=-2)
    return both.reshape(both.shape[0], WIDE, PAIR_HID)


def output_weights(bfly_out):
    straight, cross = pair_weights(bfly_out)
    upper = jnp.concatenate([straight[:, 0], cross[:, 0]], axis=-1)
    lower = jnp.concatenate([cross[:, 1], straight[:, 1]], axis=-1)
    return jnp.concatenate([upper, lower], axis=-2)


def order_matrix(order_ref, half):
    order = order_ref[0, half : half + 1, :]
    return (lax.broadcasted_iota(jnp.int32, (BLK, BLK), 0) == order).astype(jnp.bfloat16)


def widen(refs):
    return jnp.concatenate([ref[...] for ref in refs], axis=1)


def level_columns(weight_ref):
    return jnp.concatenate([weight_ref[0, source] for source in range(SOURCES)], axis=1)


def spread(result, local_count, total_ref, remote_refs):
    pair = pl.program_id(0)

    @pl.when(pair == 0)
    def _():
        total_ref[...] = jnp.zeros_like(total_ref)

    for source in range(SOURCES):
        part = result[:, source * PAIR_IN : (source + 1) * PAIR_IN]
        if source <= local_count:
            target = pair ^ (0 if source == 0 else 2 ** (source - 1))
            columns = pl.ds(pl.multiple_of(target * PAIR_IN, PAIR_IN), PAIR_IN)
            total_ref[:, columns] += part
        else:
            remote_refs[source - local_count - 1][...] = part.astype(jnp.bfloat16)


def accumulate(ref, part):
    @pl.when(pl.program_id(0) == 0)
    def _():
        ref[...] = part

    @pl.when(pl.program_id(0) > 0)
    def _():
        ref[...] += part


def forward_kernel(local_count, *refs):
    sources = refs[:SOURCES]
    in_ref, out_ref, first_ref, low_in_b_ref, low_out_a_ref, order_ref = refs[SOURCES : SOURCES + 6]
    hidden_ref, slope_ref, total_ref, second_ref = refs[SOURCES + 6 : SOURCES + 10]
    remote = refs[SOURCES + 10 :]
    pre_act = dot(widen(sources), in_ref[0], 1, 0) + dot(first_ref[...], low_in_b_ref[...], 1, 0)
    cumulative = 0.5 * (1.0 + lax.erf(pre_act * inv_root_two))
    density = jnp.exp(-0.5 * pre_act * pre_act) * inv_root_tau
    activated = (pre_act * cumulative).astype(jnp.bfloat16)
    slope = (cumulative + pre_act * density).astype(jnp.bfloat16)
    for half in range(2):
        matrix = order_matrix(order_ref, half)
        columns = slice(half * BLK, (half + 1) * BLK)
        hidden_ref[:, columns] = dot(activated[:, columns], matrix, 1, 0).astype(jnp.bfloat16)
        slope_ref[:, columns] = dot(slope[:, columns], matrix, 1, 0).astype(jnp.bfloat16)
    hidden = hidden_ref[...]
    spread(dot(hidden, level_columns(out_ref), 1, 0), local_count, total_ref, remote)
    accumulate(second_ref, dot(hidden, low_out_a_ref[...], 1, 0))


def backward_kernel(local_count, *refs):
    sources = refs[:SOURCES]
    in_ref, out_ref, second_ref, low_in_b_ref, low_out_a_ref, order_ref, slope_ref = refs[
        SOURCES : SOURCES + 7
    ]
    pre_grad_ref, total_ref, first_ref = refs[SOURCES + 7 : SOURCES + 10]
    remote = refs[SOURCES + 10 :]
    hidden_grad = dot(widen(sources), level_columns(out_ref), 1, 1) + dot(
        second_ref[...], low_out_a_ref[...], 1, 1
    )
    ordered = (hidden_grad * slope_ref[...].astype(jnp.float32)).astype(jnp.bfloat16)
    for half in range(2):
        matrix = order_matrix(order_ref, half)
        columns = slice(half * BLK, (half + 1) * BLK)
        pre_grad_ref[:, columns] = dot(ordered[:, columns], matrix, 1, 1).astype(jnp.bfloat16)
    pre_grad = pre_grad_ref[...]
    spread(dot(pre_grad, in_ref[0], 1, 1), local_count, total_ref, remote)
    accumulate(first_ref, dot(pre_grad, low_in_b_ref[...], 1, 1))


def keep_and_send(lower, upper, keep_ref, send_ref, where=...):
    second = lax.axis_index("tok") == 1
    keep_ref[where] = jnp.where(second, upper, lower)
    send_ref[where] = jnp.where(second, lower, upper).astype(jnp.bfloat16)


def tile_places():
    for half in range(2):
        yield half, 0, 0, 1 - half
        for source, level in enumerate(LEVEL_ORDER):
            yield half, level, source, half


def grad_in_kernel(scale, *refs):
    sources = refs[:SOURCES]
    pre_grad_ref, first_ref, tile_keep, tile_send, low_keep, low_send = refs[SOURCES:]
    pre_grad = pre_grad_ref[...]
    tiles = dot(widen(sources), pre_grad, 0, 0) * scale
    for half, level, source, side in tile_places():
        start = source * PAIR_IN + side * IB
        tile = tiles[start : start + IB, half * BLK : (half + 1) * BLK]
        keep_and_send(
            tile[:, : BLK // 2], tile[:, BLK // 2 :], tile_keep, tile_send, (half, level)
        )
    low = dot(first_ref[...], pre_grad, 0, 0) * scale
    middle = low.shape[0] // 2
    keep_and_send(low[:middle], low[middle:], low_keep, low_send)


def grad_out_kernel(scale, *refs):
    sources = refs[:SOURCES]
    hidden_ref, second_ref, tile_keep, tile_send, low_keep, low_send = refs[SOURCES:]
    hidden = hidden_ref[...]
    tiles = dot(hidden, widen(sources), 0, 0) * scale
    for half, level, source, side in tile_places():
        start = source * PAIR_IN + side * IB
        tile = tiles[half * BLK : (half + 1) * BLK, start : start + IB]
        keep_and_send(tile[: BLK // 2], tile[BLK // 2 :], tile_keep, tile_send, (half, level))
    low = dot(hidden, second_ref[...], 0, 0) * scale
    middle = low.shape[1] // 2
    keep_and_send(low[:, :middle], low[:, middle:], low_keep, low_send)


def call(kernel, pairs, in_specs, out_specs, out_shape, args, flops):
    size = sum(a.size * a.dtype.itemsize for a in args) + sum(
        s.size * s.dtype.itemsize for s in out_shape
    )
    return pl.pallas_call(
        kernel,
        grid=(pairs,),
        in_specs=in_specs,
        out_specs=out_specs,
        out_shape=out_shape,
        compiler_params=pltpu.CompilerParams(
            vmem_limit_bytes=VMEM_BYTES, dimension_semantics=("arbitrary",)
        ),
        cost_estimate=pl.CostEstimate(flops=flops, bytes_accessed=size, transcendentals=0),
    )(*args)


def on_device(
    tokens,
    teacher,
    assigned,
    bfly_in,
    bfly_out,
    low_in_a,
    low_in_b,
    low_out_a,
    low_out_b,
    hidden_order,
):
    rows, features = tokens.shape
    per_device = bfly_in.shape[0]
    pairs = per_device // 2
    units = per_device * BLK
    rank = low_in_a.shape[1]
    loss_scale = (rows * lax.axis_size("tok")) ** (-0.5)
    local_count = per_device.bit_length() - 2
    masks = [2**level // per_device for level in range(local_count + 1, LEVELS)]
    remote_count = len(masks)
    sds = jax.ShapeDtypeStruct
    bf16, f32 = jnp.bfloat16, jnp.float32

    def exchange(values):
        return [partner(value, "hid", mask) for value, mask in zip(values, masks)]

    feature_spec = pl.BlockSpec((rows, PAIR_IN), lambda p: (0, p))
    local_specs = [
        pl.BlockSpec((rows, PAIR_IN), functools.partial(lambda s, p: (0, p ^ s), 2**level))
        for level in range(local_count)
    ]
    source_specs = [feature_spec] + local_specs + [feature_spec] * remote_count
    unit_spec = pl.BlockSpec((rows, PAIR_HID), lambda p: (0, p))
    whole_rank = pl.BlockSpec((rows, rank), lambda p: (0, 0))
    whole_features = pl.BlockSpec((rows, features), lambda p: (0, 0))
    in_spec = pl.BlockSpec((1, WIDE, PAIR_HID), lambda p: (p, 0, 0))
    out_spec = pl.BlockSpec((1, SOURCES, PAIR_HID, PAIR_IN), lambda p: (p, 0, 0, 0))
    rank_columns = pl.BlockSpec((rank, PAIR_HID), lambda p: (0, p))
    rank_rows = pl.BlockSpec((PAIR_HID, rank), lambda p: (p, 0))
    order_spec = pl.BlockSpec((1, 2, BLK), lambda p: (p, 0, 0))
    remote_shapes = [sds((rows, features), bf16)] * remote_count
    order = hidden_order.reshape(pairs, 2, BLK)
    work = 2 * rows * units

    def with_local(own, remote):
        return [own] * (1 + local_count) + remote

    low_first = hid_sum(dot(tokens, low_in_a, 1, 0))
    token_sources = with_local(tokens, exchange([tokens] * remote_count))
    w_in = input_weights(bfly_in)
    w_out = output_weights(bfly_out)

    hidden, slope, out_total, second_part, *out_remote = call(
        functools.partial(forward_kernel, local_count),
        pairs,
        source_specs + [in_spec, out_spec, whole_rank, rank_columns, rank_rows, order_spec],
        [unit_spec, unit_spec, whole_features, whole_rank] + [feature_spec] * remote_count,
        [
            sds((rows, units), bf16),
            sds((rows, units), bf16),
            sds((rows, features), f32),
            sds((rows, rank), f32),
        ]
        + remote_shapes,
        token_sources + [w_in, w_out, low_first, low_in_b, low_out_a, order],
        work * 2 * (WIDE + rank + BLK),
    )
    low_second = hid_sum(second_part)
    student_wide = out_total + dot(low_second, low_out_b, 1, 0)
    for arrived in exchange(out_remote):
        student_wide = student_wide + arrived.astype(f32)
    student = student_wide.astype(bf16)
    residual_grad = (
        assigned[:, None].astype(f32) * (student.astype(f32) - teacher.astype(f32))
    ).astype(bf16)
    grad_second = hid_sum(dot(residual_grad, low_out_b, 1, 1))
    grad_sources = with_local(residual_grad, exchange([residual_grad] * remote_count))

    pre_grad, feat_total, first_part, *feat_remote = call(
        functools.partial(backward_kernel, local_count),
        pairs,
        source_specs
        + [in_spec, out_spec, whole_rank, rank_columns, rank_rows, order_spec, unit_spec],
        [unit_spec, whole_features, whole_rank] + [feature_spec] * remote_count,
        [sds((rows, units), bf16), sds((rows, features), f32), sds((rows, rank), f32)]
        + remote_shapes,
        grad_sources + [w_in, w_out, grad_second, low_in_b, low_out_a, order, slope],
        work * 2 * (WIDE + rank + BLK // 2),
    )
    feat_arrived = exchange(feat_remote)
    grad_first = hid_sum(first_part)

    tile_in = pl.BlockSpec((2, LEVELS + 1, IB, BLK // 2), lambda p: (p, 0, 0, 0))
    low_in = pl.BlockSpec((rank // 2, PAIR_HID), lambda p: (0, p))
    tile_out = pl.BlockSpec((2, LEVELS + 1, BLK // 2, IB), lambda p: (p, 0, 0, 0))
    low_out = pl.BlockSpec((PAIR_HID, rank // 2), lambda p: (p, 0))
    tile_in_dims = (per_device, LEVELS + 1, IB, BLK // 2)
    tile_out_dims = (per_device, LEVELS + 1, BLK // 2, IB)
    kept_out = call(
        functools.partial(grad_out_kernel, loss_scale),
        pairs,
        source_specs + [unit_spec, whole_rank],
        [tile_out, tile_out, low_out, low_out],
        [
            sds(tile_out_dims, f32),
            sds(tile_out_dims, bf16),
            sds((units, rank // 2), f32),
            sds((units, rank // 2), bf16),
        ],
        grad_sources + [hidden, grad_second],
        work * (WIDE + rank),
    )
    kept_in = call(
        functools.partial(grad_in_kernel, loss_scale),
        pairs,
        source_specs + [unit_spec, whole_rank],
        [tile_in, tile_in, low_in, low_in],
        [
            sds(tile_in_dims, f32),
            sds(tile_in_dims, bf16),
            sds((rank // 2, units), f32),
            sds((rank // 2, units), bf16),
        ],
        token_sources + [pre_grad, low_first],
        work * (WIDE + rank),
    )

    def tok_sum(keep, send):
        return keep + partner(send, "tok", 1).astype(f32)

    def tok_halves(value, axis):
        low, high = jnp.split(value, 2, axis=axis)
        second = lax.axis_index("tok") == 1
        return tok_sum(
            jnp.where(second, high, low), jnp.where(second, low, high).astype(bf16)
        )

    grad_low_out_b = tok_halves(dot(low_second, residual_grad, 0, 0) * loss_scale, 0)
    grad_bfly_out = tok_sum(kept_out[0], kept_out[1])
    grad_low_out_a = tok_sum(kept_out[2], kept_out[3])
    grad_bfly_in = tok_sum(kept_in[0], kept_in[1])
    grad_low_in_b = tok_sum(kept_in[2], kept_in[3])
    grad_low_in_a = tok_halves(dot(tokens, grad_first, 0, 0) * loss_scale, 1)
    feat = feat_total + dot(grad_first, low_in_a, 1, 1)
    for arrived in feat_arrived:
        feat = feat + arrived.astype(f32)
    grad_tokens = feat.astype(bf16)
    return (
        student,
        grad_tokens,
        grad_bfly_in,
        grad_bfly_out,
        grad_low_in_a,
        grad_low_in_b,
        grad_low_out_a,
        grad_low_out_b,
    )


def solution(mesh):
    placed = (
        P(("pop", "tok"), "hid"),
        P(("pop", "tok"), "hid"),
        P(("pop", "tok")),
        P(("pop", "hid"), None, None, None),
        P(("pop", "hid"), None, None, None),
        P(("pop", "hid"), None),
        P("pop", "hid"),
        P(("pop", "hid"), None),
        P("pop", "hid"),
        P("hid", None),
    )
    return jax.shard_map(
        on_device,
        mesh=mesh,
        in_specs=placed,
        out_specs=(
            P(("pop", "tok"), "hid"),
            P(("pop", "tok"), "hid"),
            P(("pop", "hid"), None, None, "tok"),
            P(("pop", "hid"), None, "tok", None),
            P(("pop", "hid"), "tok"),
            P(("pop", "tok"), "hid"),
            P(("pop", "hid"), "tok"),
            P(("pop", "tok"), "hid"),
        ),
        check_vma=False,
    )
```

```python
import functools

import jax
import jax.numpy as jnp
from jax import lax
from jax.experimental import pallas as pl
from jax.experimental.pallas import tpu as pltpu
from jax.sharding import PartitionSpec as P

BLK = 256
LEVELS = 7
IB = 64
PAIR_IN = 2 * IB
PAIR_HID = 2 * BLK
SOURCES = LEVELS
LEVEL_ORDER = (LEVELS,) + tuple(range(1, LEVELS))
WIDE = SOURCES * PAIR_IN
VMEM_BYTES = 52 * 2**20

inv_root_two = 0.7071067811865476
inv_root_tau = 0.3989422804014327


def partner(value, axis, mask):
    pairs = [(source, source ^ mask) for source in range(lax.axis_size(axis))]
    return lax.ppermute(value, axis, pairs)


def dot(left, right, left_dim, right_dim):
    return lax.dot_general(
        left, right, (((left_dim,), (right_dim,)), ((), ())), preferred_element_type=jnp.float32
    )


def hid_sum(value, arrived):
    devices = lax.axis_size("hid")
    place = lax.axis_index("hid")
    masks = [2**bit for bit in range(devices.bit_length() - 1)]
    for mask in masks:
        low, high = jnp.split(value, 2, axis=0)
        upper = (place & mask) != 0
        kept = jnp.where(upper, high, low)
        sent = jnp.where(upper, low, high).astype(jnp.bfloat16)
        value = kept + partner(sent, "hid", mask).astype(jnp.float32)
    nothing = jnp.minimum(jnp.abs(arrived[:1, :1].astype(jnp.float32)), 0.0)
    value = (value + nothing).astype(jnp.bfloat16)
    for mask in reversed(masks):
        other = partner(value, "hid", mask)
        upper = (place & mask) != 0
        value = jnp.concatenate(
            [jnp.where(upper, other, value), jnp.where(upper, value, other)], axis=0
        )
    return value


def place_tiles(tiles_ref, weight_ref):
    @pl.when(pl.program_id(0) == 0)
    def _():
        weight_ref[...] = jnp.zeros_like(weight_ref)

    for half, level, source, side in tile_places():
        start = source * PAIR_IN + side * IB
        weight_ref[start : start + IB, half * BLK : (half + 1) * BLK] = tiles_ref[half, level]


def order_matrix(order_ref, half):
    order = order_ref[0, half : half + 1, :]
    return (lax.broadcasted_iota(jnp.int32, (BLK, BLK), 0) == order).astype(jnp.bfloat16)


def widen(refs):
    return jnp.concatenate([ref[...] for ref in refs], axis=1)


def spread(result, local_count, total_ref, remote_refs):
    pair = pl.program_id(0)

    @pl.when(pair == 0)
    def _():
        total_ref[...] = jnp.zeros_like(total_ref)

    for source in range(SOURCES):
        part = result[:, source * PAIR_IN : (source + 1) * PAIR_IN]
        if source <= local_count:
            target = pair ^ (0 if source == 0 else 2 ** (source - 1))
            columns = pl.ds(pl.multiple_of(target * PAIR_IN, PAIR_IN), PAIR_IN)
            total_ref[:, columns] += part
        else:
            remote_refs[source - local_count - 1][...] = part.astype(jnp.bfloat16)


def accumulate(ref, part):
    @pl.when(pl.program_id(0) == 0)
    def _():
        ref[...] = part

    @pl.when(pl.program_id(0) > 0)
    def _():
        ref[...] += part


def forward_kernel(local_count, *refs):
    sources = refs[:SOURCES]
    in_ref, out_ref, first_ref, low_in_b_ref, low_out_a_ref, order_ref = refs[SOURCES : SOURCES + 6]
    hidden_ref, slope_ref, total_ref, second_ref = refs[SOURCES + 6 : SOURCES + 10]
    remote, (w_in, w_out) = refs[SOURCES + 10 : -2], refs[-2:]
    place_tiles(in_ref, w_in)
    place_tiles(out_ref, w_out)
    pre_act = dot(widen(sources), w_in[...], 1, 0) + dot(first_ref[...], low_in_b_ref[...], 1, 0)
    cumulative = 0.5 * (1.0 + lax.erf(pre_act * inv_root_two))
    density = jnp.exp(-0.5 * pre_act * pre_act) * inv_root_tau
    activated = (pre_act * cumulative).astype(jnp.bfloat16)
    slope = (cumulative + pre_act * density).astype(jnp.bfloat16)
    for half in range(2):
        matrix = order_matrix(order_ref, half)
        columns = slice(half * BLK, (half + 1) * BLK)
        hidden_ref[:, columns] = dot(activated[:, columns], matrix, 1, 0).astype(jnp.bfloat16)
        slope_ref[:, columns] = dot(slope[:, columns], matrix, 1, 0).astype(jnp.bfloat16)
    hidden = hidden_ref[...]
    spread(dot(hidden, w_out[...], 1, 1), local_count, total_ref, remote)
    accumulate(second_ref, dot(hidden, low_out_a_ref[...], 1, 0))


def backward_kernel(local_count, *refs):
    sources = refs[:SOURCES]
    in_ref, out_ref, second_ref, low_in_b_ref, low_out_a_ref, order_ref, slope_ref = refs[
        SOURCES : SOURCES + 7
    ]
    pre_grad_ref, total_ref, first_ref = refs[SOURCES + 7 : SOURCES + 10]
    remote, (w_in, w_out) = refs[SOURCES + 10 : -2], refs[-2:]
    place_tiles(in_ref, w_in)
    place_tiles(out_ref, w_out)
    hidden_grad = dot(widen(sources), w_out[...], 1, 0) + dot(
        second_ref[...], low_out_a_ref[...], 1, 1
    )
    ordered = (hidden_grad * slope_ref[...].astype(jnp.float32)).astype(jnp.bfloat16)
    for half in range(2):
        matrix = order_matrix(order_ref, half)
        columns = slice(half * BLK, (half + 1) * BLK)
        pre_grad_ref[:, columns] = dot(ordered[:, columns], matrix, 1, 1).astype(jnp.bfloat16)
    pre_grad = pre_grad_ref[...]
    spread(dot(pre_grad, w_in[...], 1, 1), local_count, total_ref, remote)
    accumulate(first_ref, dot(pre_grad, low_in_b_ref[...], 1, 1))


def keep_and_send(lower, upper, keep_ref, send_ref, where=...):
    second = lax.axis_index("tok") == 1
    keep_ref[where] = jnp.where(second, upper, lower)
    send_ref[where] = jnp.where(second, lower, upper).astype(jnp.bfloat16)


def tile_places():
    for half in range(2):
        yield half, 0, 0, 1 - half
        for source, level in enumerate(LEVEL_ORDER):
            yield half, level, source, half


def keep_tiles(scale, sources, unit_values, tile_keep, tile_send):
    tiles = dot(widen(sources), unit_values, 0, 0) * scale
    for half, level, source, side in tile_places():
        start = source * PAIR_IN + side * IB
        tile = tiles[start : start + IB, half * BLK : (half + 1) * BLK]
        keep_and_send(
            tile[:, : BLK // 2], tile[:, BLK // 2 :], tile_keep, tile_send, (half, level)
        )


def grad_in_kernel(scale, *refs):
    pre_grad_ref, first_ref, tile_keep, tile_send, low_keep, low_send = refs[SOURCES:]
    pre_grad = pre_grad_ref[...]
    keep_tiles(scale, refs[:SOURCES], pre_grad, tile_keep, tile_send)
    low = dot(first_ref[...], pre_grad, 0, 0) * scale
    middle = low.shape[0] // 2
    keep_and_send(low[:middle], low[middle:], low_keep, low_send)


def grad_out_kernel(scale, *refs):
    hidden_ref, second_ref, tile_keep, tile_send, low_keep, low_send = refs[SOURCES:]
    hidden = hidden_ref[...]
    keep_tiles(scale, refs[:SOURCES], hidden, tile_keep, tile_send)
    low = dot(hidden, second_ref[...], 0, 0) * scale
    middle = low.shape[1] // 2
    keep_and_send(low[:, :middle], low[:, middle:], low_keep, low_send)


def call(kernel, pairs, in_specs, out_specs, out_shape, args, flops, scratch=()):
    size = sum(a.size * a.dtype.itemsize for a in args) + sum(
        s.size * s.dtype.itemsize for s in out_shape
    )
    return pl.pallas_call(
        kernel,
        grid=(pairs,),
        in_specs=in_specs,
        out_specs=out_specs,
        out_shape=out_shape,
        scratch_shapes=scratch,
        compiler_params=pltpu.CompilerParams(
            vmem_limit_bytes=VMEM_BYTES, dimension_semantics=("arbitrary",)
        ),
        cost_estimate=pl.CostEstimate(flops=flops, bytes_accessed=size, transcendentals=0),
    )(*args)


def on_device(
    tokens,
    teacher,
    assigned,
    bfly_in,
    bfly_out,
    low_in_a,
    low_in_b,
    low_out_a,
    low_out_b,
    hidden_order,
):
    rows, features = tokens.shape
    per_device = bfly_in.shape[0]
    pairs = per_device // 2
    units = per_device * BLK
    rank = low_in_a.shape[1]
    loss_scale = (rows * lax.axis_size("tok")) ** (-0.5)
    local_count = per_device.bit_length() - 2
    masks = [2**level // per_device for level in range(local_count + 1, LEVELS)]
    remote_count = len(masks)
    sds = jax.ShapeDtypeStruct
    bf16, f32 = jnp.bfloat16, jnp.float32

    def exchange(values):
        return [partner(value, "hid", mask) for value, mask in zip(values, masks)]

    feature_spec = pl.BlockSpec((rows, PAIR_IN), lambda p: (0, p))
    local_specs = [
        pl.BlockSpec((rows, PAIR_IN), functools.partial(lambda s, p: (0, p ^ s), 2**level))
        for level in range(local_count)
    ]
    source_specs = [feature_spec] + local_specs + [feature_spec] * remote_count
    unit_spec = pl.BlockSpec((rows, PAIR_HID), lambda p: (0, p))
    whole_rank = pl.BlockSpec((rows, rank), lambda p: (0, 0))
    whole_features = pl.BlockSpec((rows, features), lambda p: (0, 0))
    tile_spec = pl.BlockSpec((2, LEVELS + 1, IB, BLK), lambda p: (p, 0, 0, 0))
    weight_scratch = [pltpu.VMEM((WIDE, PAIR_HID), bf16)] * 2
    rank_columns = pl.BlockSpec((rank, PAIR_HID), lambda p: (0, p))
    rank_rows = pl.BlockSpec((PAIR_HID, rank), lambda p: (p, 0))
    order_spec = pl.BlockSpec((1, 2, BLK), lambda p: (p, 0, 0))
    remote_shapes = [sds((rows, features), bf16)] * remote_count
    order = hidden_order.reshape(pairs, 2, BLK)
    work = 2 * rows * units

    def with_local(own, remote):
        return [own] * (1 + local_count) + remote

    token_sources = with_local(tokens, exchange([tokens] * remote_count))
    low_first = hid_sum(dot(tokens, low_in_a, 1, 0), token_sources[-1])
    out_tiles = jnp.swapaxes(bfly_out, 2, 3)

    hidden, slope, out_total, second_part, *out_remote = call(
        functools.partial(forward_kernel, local_count),
        pairs,
        source_specs + [tile_spec, tile_spec, whole_rank, rank_columns, rank_rows, order_spec],
        [unit_spec, unit_spec, whole_features, whole_rank] + [feature_spec] * remote_count,
        [
            sds((rows, units), bf16),
            sds((rows, units), bf16),
            sds((rows, features), f32),
            sds((rows, rank), f32),
        ]
        + remote_shapes,
        token_sources + [bfly_in, out_tiles, low_first, low_in_b, low_out_a, order],
        work * 2 * (WIDE + rank + BLK),
        weight_scratch,
    )
    out_arrived = exchange(out_remote)
    low_second = hid_sum(second_part, out_arrived[-1])
    student_wide = out_total + dot(low_second, low_out_b, 1, 0)
    for arrived in out_arrived:
        student_wide = student_wide + arrived.astype(f32)
    student = student_wide.astype(bf16)
    residual_grad = (
        assigned[:, None].astype(f32) * (student.astype(f32) - teacher.astype(f32))
    ).astype(bf16)
    grad_sources = with_local(residual_grad, exchange([residual_grad] * remote_count))
    grad_second = hid_sum(dot(residual_grad, low_out_b, 1, 1), grad_sources[-1])

    pre_grad, feat_total, first_part, *feat_remote = call(
        functools.partial(backward_kernel, local_count),
        pairs,
        source_specs
        + [tile_spec, tile_spec, whole_rank, rank_columns, rank_rows, order_spec, unit_spec],
        [unit_spec, whole_features, whole_rank] + [feature_spec] * remote_count,
        [sds((rows, units), bf16), sds((rows, features), f32), sds((rows, rank), f32)]
        + remote_shapes,
        grad_sources + [bfly_in, out_tiles, grad_second, low_in_b, low_out_a, order, slope],
        work * 2 * (WIDE + rank + BLK // 2),
        weight_scratch,
    )
    feat_arrived = exchange(feat_remote)
    grad_first = hid_sum(first_part, feat_arrived[-1])

    tile_in = pl.BlockSpec((2, LEVELS + 1, IB, BLK // 2), lambda p: (p, 0, 0, 0))
    low_in = pl.BlockSpec((rank // 2, PAIR_HID), lambda p: (0, p))
    low_out = pl.BlockSpec((PAIR_HID, rank // 2), lambda p: (p, 0))
    tile_in_dims = (per_device, LEVELS + 1, IB, BLK // 2)
    kept_out = call(
        functools.partial(grad_out_kernel, loss_scale),
        pairs,
        source_specs + [unit_spec, whole_rank],
        [tile_in, tile_in, low_out, low_out],
        [
            sds(tile_in_dims, f32),
            sds(tile_in_dims, bf16),
            sds((units, rank // 2), f32),
            sds((units, rank // 2), bf16),
        ],
        grad_sources + [hidden, grad_second],
        work * (WIDE + rank),
    )
    kept_in = call(
        functools.partial(grad_in_kernel, loss_scale),
        pairs,
        source_specs + [unit_spec, whole_rank],
        [tile_in, tile_in, low_in, low_in],
        [
            sds(tile_in_dims, f32),
            sds(tile_in_dims, bf16),
            sds((rank // 2, units), f32),
            sds((rank // 2, units), bf16),
        ],
        token_sources + [pre_grad, low_first],
        work * (WIDE + rank),
    )

    def tok_sum(keep, send):
        return keep + partner(send, "tok", 1).astype(f32)

    def tok_halves(value, axis):
        low, high = jnp.split(value, 2, axis=axis)
        second = lax.axis_index("tok") == 1
        return tok_sum(
            jnp.where(second, high, low), jnp.where(second, low, high).astype(bf16)
        )

    grad_low_out_b = tok_halves(dot(low_second, residual_grad, 0, 0) * loss_scale, 0)
    grad_bfly_out = jnp.swapaxes(tok_sum(kept_out[0], kept_out[1]), 2, 3)
    grad_low_out_a = tok_sum(kept_out[2], kept_out[3])
    grad_bfly_in = tok_sum(kept_in[0], kept_in[1])
    grad_low_in_b = tok_sum(kept_in[2], kept_in[3])
    grad_low_in_a = tok_halves(dot(tokens, grad_first, 0, 0) * loss_scale, 1)
    feat = feat_total + dot(grad_first, low_in_a, 1, 1)
    for arrived in feat_arrived:
        feat = feat + arrived.astype(f32)
    grad_tokens = feat.astype(bf16)
    return (
        student,
        grad_tokens,
        grad_bfly_in,
        grad_bfly_out,
        grad_low_in_a,
        grad_low_in_b,
        grad_low_out_a,
        grad_low_out_b,
    )


def solution(mesh):
    placed = (
        P(("pop", "tok"), "hid"),
        P(("pop", "tok"), "hid"),
        P(("pop", "tok")),
        P(("pop", "hid"), None, None, None),
        P(("pop", "hid"), None, None, None),
        P(("pop", "hid"), None),
        P("pop", "hid"),
        P(("pop", "hid"), None),
        P("pop", "hid"),
        P("hid", None),
    )
    return jax.shard_map(
        on_device,
        mesh=mesh,
        in_specs=placed,
        out_specs=(
            P(("pop", "tok"), "hid"),
            P(("pop", "tok"), "hid"),
            P(("pop", "hid"), None, None, "tok"),
            P(("pop", "hid"), None, "tok", None),
            P(("pop", "hid"), "tok"),
            P(("pop", "tok"), "hid"),
            P(("pop", "hid"), "tok"),
            P(("pop", "tok"), "hid"),
        ),
        check_vma=False,
    )
```
